32 devices in a mesh: ty: 4 (over x, core), tx: 2 (over y), ta: 4 (over z).
Axes of the slice: x: 2, y: 2, z: 4, core: 2. Of those that a mesh axis runs over, the one named last changes fastest.
Arguments:
- movie: bfloat16 [16, 4, 1024, 256], P('ta', None, 'ty', 'tx'), may hold values from 0 to 2
- footprints: float32 [512, 4096], P(('ty', 'tx')), may hold values from 0 to 1
- traces: float32 [16, 512], P('ta', ('ty', 'tx')), may hold values from 0 to 1
- anchor_row: int32 [512], P(('ty', 'tx')), may hold values from -1 to 15
- anchor_col: int32 [512], P(('ty', 'tx')), may hold values from -1 to 7
Outputs:
- footprints_out: float32 [512, 4096], P(('ty', 'tx'))
- traces_out: float32 [16, 512], P('ta', ('ty', 'tx'))
The draws below stay inside these ranges and needn't reach their ends.
Inputs may be any that keep to these rules, and one draw needn't show every extreme that they name: `anchor_row`: cell row within the owner tile at which a neuron's patch block starts; -1 puts its upper half into the tile above. `anchor_col`: cell column within the owner tile at which a neuron's patch block starts; -1 puts its left half into the tile beside it.
All inputs are finite; a program needn't handle non-finite values.
Results may differ from the reference program's by a relative error of at most 0.0003.
Values may be sent and summed in bfloat16 or wider, within the bound.
A program may use at most 128 MiB of HBM per device.

```python
import jax
import jax.numpy as jnp
from jax import lax

CELL = 16
PZ = 4
CY = 16
CX = 8
K_DEV = 64
ITERS = 2
PATCH = 4096
NEURONS = 512
FRAMES = 16
NY = 1024
NX = 256
N_TX = 2


def set_ends(entries, rng, least, high):
    index_at = [jax.random.randint(jax.random.fold_in(rng, axis), (), 0, length) for axis, length in enumerate(entries.shape)]
    main_axis = entries.shape.index(max(entries.shape))
    beside = index_at[:main_axis] + [(index_at[main_axis] + 1) % entries.shape[main_axis]] + index_at[main_axis + 1:]
    return entries.at[tuple(index_at)].set(least).at[tuple(beside)].set(high)


def shard_levels(own_key, shape, split, smallest, largest):
    loudness = 1.0
    for axis_at, shards_of in split:
        steps = jax.random.uniform(jax.random.fold_in(jax.random.fold_in(own_key, 6), axis_at), (shards_of,), jnp.float32, smallest / len(split), largest / len(split))
        loudness = loudness * jnp.repeat(jnp.exp(steps), shape[axis_at] // shards_of).reshape((-1,) + (1,) * (len(shape) - 1 - axis_at))
    return loudness


def setup_inputs(seed: int = 0) -> dict:
    streams_of = jax.random.split(jax.random.key(seed), 6)
    return {
        "movie": jnp.clip(2.0 * jax.random.uniform(streams_of[0], (FRAMES, PZ, NY, NX), jnp.float32) ** shard_levels(streams_of[0], (FRAMES, PZ, NY, NX), ((0, 4), (2, 4), (3, 2)), -0.2, 0.2), 0.0, 2.0).astype(jnp.bfloat16),
        "footprints": jnp.clip(1.0 * jax.random.uniform(streams_of[1], (NEURONS, PATCH), jnp.float32) ** shard_levels(streams_of[1], (NEURONS, PATCH), ((0, 8),), -0.2, 0.2), 0.0, 1.0),
        "traces": jnp.clip(1.0 * jax.random.uniform(streams_of[2], (FRAMES, NEURONS), jnp.float32) ** shard_levels(streams_of[2], (FRAMES, NEURONS), ((0, 4), (1, 8)), -0.2, 0.2), 0.0, 1.0),
        "anchor_row": set_ends(jax.random.randint(streams_of[3], (NEURONS,), -1, CY), jax.random.fold_in(streams_of[3], 1), -1, CY - 1).astype(jnp.int32),
        "anchor_col": set_ends(jax.random.randint(streams_of[4], (NEURONS,), -1, CX), jax.random.fold_in(streams_of[4], 1), -1, CX - 1).astype(jnp.int32),
    }


RIDGE = 1.0


def cell_lists(anchor_row, anchor_col):
    neuron_ids = jnp.arange(NEURONS, dtype=jnp.int32)
    tile_row = neuron_ids // (K_DEV * N_TX)
    tile_col = (neuron_ids // K_DEV) % N_TX
    grid_cols = CX * N_TX + 2
    top_cell = tile_row * CY + anchor_row.astype(jnp.int32) + 1
    left_cell = tile_col * CX + anchor_col.astype(jnp.int32) + 1
    corner = top_cell * grid_cols + left_cell
    offsets = jnp.array([0, 1, grid_cols, grid_cols + 1], dtype=jnp.int32)
    return (corner[:, None] + offsets[None, :]).reshape(-1)


def frame_cells(movie_frame):
    padded = jnp.pad(movie_frame.astype(jnp.float32), ((0, 0), (CELL, CELL), (CELL, CELL)))
    grid_rows = NY // CELL + 2
    grid_cols = NX // CELL + 2
    blocks = padded.reshape(PZ, grid_rows, CELL, grid_cols, CELL).transpose(1, 3, 0, 2, 4)
    return blocks.reshape(grid_rows * grid_cols, PZ * CELL * CELL)


def frame_residue(movie_frame, trace_row, footprints, cell_ids, cell_total):
    products = footprints.reshape(NEURONS, 4, PZ * CELL * CELL) * trace_row[:, None, None]
    estimate = jax.ops.segment_sum(products.reshape(NEURONS * 4, -1), cell_ids, num_segments=cell_total)
    residue = frame_cells(movie_frame) - estimate
    return jnp.take(residue, cell_ids, axis=0).reshape(NEURONS, PATCH)


def reference(movie, footprints, traces, anchor_row, anchor_col):
    cell_ids = cell_lists(anchor_row, anchor_col)
    cell_total = (NY // CELL + 2) * (NX // CELL + 2)
    for sweep in range(ITERS):
        energy = jnp.sum(footprints * footprints, axis=1)

        def trace_frame(inputs):
            movie_frame, trace_row = inputs
            gathered = frame_residue(movie_frame, trace_row, footprints, cell_ids, cell_total)
            update = jnp.sum(footprints * gathered, axis=1)
            return jnp.maximum(trace_row + update / (energy + RIDGE), 0.0)

        traces = lax.map(trace_frame, (movie, traces))

        def foot_frame(running, inputs):
            movie_frame, trace_row = inputs
            gathered = frame_residue(movie_frame, trace_row, footprints, cell_ids, cell_total)
            return running + trace_row[:, None] * gathered, None

        numerator, _ = lax.scan(foot_frame, jnp.zeros((NEURONS, PATCH), jnp.float32), (movie, traces))
        strength = jnp.sum(traces * traces, axis=0)
        footprints = jnp.maximum(footprints + numerator / (strength + RIDGE)[:, None], 0.0)
    return footprints, traces
```

```python
import jax
import jax.numpy as jnp
from jax import lax
from jax.sharding import PartitionSpec as P

CELL = 16
ITERS = 2
RIDGE = 1.0
HI = lax.Precision.HIGHEST


def steps(count):
    if count == 1:
        return []
    if count == 2:
        return [[(0, 1), (1, 0)]]
    return [
        [(i, i + 1) for i in range(count - 1)],
        [(i + 1, i) for i in range(count - 1)],
    ]


def around(x):
    for axis in ("tx", "ty"):
        x = jnp.concatenate(
            [x] + [lax.ppermute(x, axis, pairs) for pairs in steps(lax.axis_size(axis))]
        )
    return x


def with_halo(cells, sides, width):
    for axis, dim in sides:
        count = lax.axis_size(axis)
        ends = count - 1
        head = lax.slice_in_dim(cells, 0, width, axis=dim)
        tail = lax.slice_in_dim(cells, cells.shape[dim] - width, cells.shape[dim], axis=dim)
        cells = jnp.concatenate(
            [
                lax.ppermute(tail, axis, [(i, (i + 1) % count) for i in range(ends)]),
                cells,
                lax.ppermute(head, axis, [((i + 1) % count, i) for i in range(ends)]),
            ],
            axis=dim,
        )
    return cells


def shards(movie, footprints, traces, anchor_row, anchor_col):
    owned = footprints.shape[0]
    frames, planes, height, breadth = movie.shape
    rows, cols = height // CELL, breadth // CELL
    spot = CELL * CELL
    groups = lax.axis_size("ta")
    mine = planes // groups
    part = mine * spot
    cells = movie.reshape(frames, planes, rows, CELL, cols, CELL).transpose(0, 1, 2, 4, 3, 5)
    cells = cells.reshape(frames, planes, rows, cols, spot)
    cells = lax.all_to_all(cells, "ta", split_axis=1, concat_axis=0, tiled=True)
    cells = with_halo(cells, (("ty", 2), ("tx", 3)), 1)
    frames = frames * groups
    grid = (rows + 2) * (cols + 2)
    cells = cells.transpose(0, 2, 3, 1, 4).reshape(frames, grid, part)
    width = cols * lax.axis_size("tx") + 2
    top = lax.axis_index("ty") * rows
    left = lax.axis_index("tx") * cols
    first = (anchor_row + 1 + top) * width + anchor_col + 1 + left
    offsets = jnp.array([0, 1, width, width + 1], dtype=jnp.int32)
    ids = (offsets[:, None] + first[None, :]).reshape(1, -1).astype(jnp.float32)
    place = (
        (jnp.arange(rows + 2) + top)[:, None] * width + (jnp.arange(cols + 2) + left)[None, :]
    ).reshape(-1, 1).astype(jnp.float32)
    on_cell = place == ids
    rank = lax.axis_index("ta")
    feet = lax.dynamic_slice_in_dim(
        footprints.reshape(owned, 4, planes, spot), rank * mine, mine, axis=2
    )
    feet = feet.transpose(1, 0, 2, 3).reshape(4 * owned, part)
    marks = lax.all_gather(traces, "ta", axis=0, tiled=True)
    times = jnp.tile(marks, (1, 4))
    small = around(jnp.concatenate([times, ids])[None])
    all_times, all_ids = small[:, :-1], small[:, -1:]
    same = ids.reshape(-1, 1)[None] == all_ids
    for sweep in range(ITERS):
        energy = jnp.sum(feet * feet, axis=1).reshape(4, owned).sum(axis=0)
        all_feet = around(feet[None])
        over = jnp.where(same, jnp.einsum("ae,tbe->tab", feet, all_feet, precision=HI), 0.0)
        seen = jnp.einsum("fce,ae->fca", cells.astype(jnp.float32), feet, precision=HI)
        seen = jnp.where(on_cell[None], seen, 0.0).sum(axis=1)
        update = seen - jnp.einsum("tfb,tab->fa", all_times, over, precision=HI)
        update = update.reshape(frames, 4, owned).sum(axis=1)
        total = lax.psum(jnp.concatenate([update, energy[None]]), "ta")
        marks = jnp.maximum(marks + total[:-1] / (total[-1:] + RIDGE), 0.0)
        times = jnp.tile(marks, (1, 4))
        all_times = around(times[None])
        strength = jnp.sum(times * times, axis=0)
        spread = jnp.where(on_cell[None], times[:, None, :], 0.0)
        numer = jnp.einsum("fca,fce->ae", spread, cells.astype(jnp.float32), precision=HI)
        both = jnp.where(same, jnp.einsum("fa,tfb->tab", times, all_times, precision=HI), 0.0)
        numer = numer - jnp.einsum("tab,tbe->ae", both, all_feet, precision=HI)
        feet = jnp.maximum(feet + numer / (strength + RIDGE)[:, None], 0.0)
    feet = feet.reshape(4, owned, mine, spot).transpose(1, 0, 2, 3)
    feet = lax.all_gather(feet, "ta", axis=2, tiled=True).reshape(owned, -1)
    own_frames = marks.shape[0] // groups
    return feet, lax.dynamic_slice_in_dim(marks, rank * own_frames, own_frames, axis=0)


def solution(mesh):
    placed = (
        P("ta", None, "ty", "tx"),
        P(("ty", "tx"), None),
        P("ta", ("ty", "tx")),
        P(("ty", "tx")),
        P(("ty", "tx")),
    )
    return jax.shard_map(
        shards,
        mesh=mesh,
        in_specs=placed,
        out_specs=(P(("ty", "tx"), None), P("ta", ("ty", "tx"))),
        check_vma=False,
    )
```

```python
import functools

import jax
import jax.numpy as jnp
from jax import lax
from jax.experimental import pallas as pl
from jax.experimental.pallas import tpu as pltpu
from jax.sharding import PartitionSpec as P

CELL = 16
ITERS = 2
RIDGE = 1.0
HI = lax.Precision.HIGHEST
F32 = jnp.float32
BF16 = jnp.bfloat16
MESH = pl.DeviceIdType.MESH


def reach(count):
    return [0] if count == 1 else [0, 1] if count == 2 else [0, -1, 1]


def directions(mesh_y, mesh_x):
    return [(dy, dx) for dy in reach(mesh_y) for dx in reach(mesh_x)]


def shift(at, count, d):
    if d == 0:
        return at, None
    if count == 2:
        return 1 - at, None
    to = at + d
    return to, (to >= 0) & (to < count)


def opposite(d, count):
    return d if count == 2 else -d


def thirds(x):
    high = x.astype(BF16)
    rest = x - high.astype(F32)
    middle = rest.astype(BF16)
    return high, middle, (rest - middle.astype(F32)).astype(BF16)


def nt(a, b):
    return lax.dot_general(a, b, (((1,), (1,)), ((), ())), precision=HI, preferred_element_type=F32)


def nn(a, b):
    return jnp.dot(a, b, precision=HI, preferred_element_type=F32)


def kernel(
    sizes, movie, foot, trace, idrow, idcol, place, placerow,
    foot_out, trace_out,
    seen, cut, patch, foot_at, info_at, times_at, trace_at, part_at, feet_t, numer,
    s_mov, r_mov, s_cut, r_cut, s_foot, r_foot, s_tr, r_tr, s_info, r_info,
    s_time, r_time, s_part, r_part, s_out, r_out, l_sem,
):
    ny, nx, nz, rows, cols, local, planes, owned = sizes
    frames = local * nz
    spot = CELL * CELL
    lanes = 4 * owned
    strip = cut.shape[2]
    iy, ix, iz = lax.axis_index("ty"), lax.axis_index("tx"), lax.axis_index("ta")
    dirs = directions(ny, nx)
    slots = len(dirs)

    near = []
    for j, (dy, dx) in enumerate(dirs):
        ty, ey = shift(iy, ny, dy)
        tx, ex = shift(ix, nx, dx)
        exists = ey if ex is None else ex if ey is None else ey & ex
        back = dirs.index((opposite(dy, ny), opposite(dx, nx)))
        near.append(((ty, tx, iz), exists, back))

    def when(exists, act):
        if exists is None:
            act()
        else:
            pl.when(exists)(act)

    def far(o):
        return (iy, ix, lax.rem(iz + o, nz))

    def spread(src, dst, ssem, rsem):
        def go(j):
            device, exists, back = near[j]
            when(exists, lambda: pltpu.make_async_remote_copy(
                src_ref=src(j), dst_ref=dst(back), send_sem=ssem.at[j], recv_sem=rsem.at[back],
                device_id=device, device_id_type=MESH).start())
        for j in range(1, slots):
            go(j)

    def await_near(j, dst, ssem, rsem, send=False):
        device, exists, _ = near[j]

        def act():
            copy = pltpu.make_async_remote_copy(
                src_ref=dst, dst_ref=dst, send_sem=ssem.at[j], recv_sem=rsem.at[j],
                device_id=device, device_id_type=MESH)
            copy.wait_send() if send else copy.wait_recv()

        when(exists, act)

    def to_far(o, src, dst, ssem, rsem):
        return pltpu.make_async_remote_copy(
            src_ref=src, dst_ref=dst, send_sem=ssem, recv_sem=rsem,
            device_id=far(o), device_id_type=MESH)

    barrier = pltpu.get_barrier_semaphore()
    due = jnp.int32(nz - 1)
    for o in range(1, nz):
        pl.semaphore_signal(barrier, inc=1, device_id=far(o), device_id_type=MESH)
    for j in range(1, slots):
        device, exists, _ = near[j]
        when(exists, lambda device=device: pl.semaphore_signal(
            barrier, inc=1, device_id=device, device_id_type=MESH))
        due = due + (1 if exists is None else exists.astype(jnp.int32))
    pl.semaphore_wait(barrier, due)

    for o in range(1, nz):
        to_far(o, trace, trace_at.at[iz], s_tr.at[o], r_tr.at[o]).start()
    for o in range(1, nz):
        to_far(o, movie.at[lax.rem(iz + o, nz)], seen.at[pl.ds(iz * local, local)],
               s_mov.at[o], r_mov.at[o]).start()
    own = pltpu.make_async_copy(movie.at[iz], seen.at[pl.ds(iz * local, local)], l_sem)
    own.start()
    trace_at[iz] = trace[...]
    for s in range(4):
        first = pl.multiple_of((s * planes + iz) * spot, spot)
        foot_at[0, 0, s * owned:(s + 1) * owned, :] = foot[:, pl.ds(first, spot)]
    spread(lambda j: foot_at.at[0, 0], lambda b: foot_at.at[0, b], s_foot.at[0], r_foot.at[0])

    for j in range(1, slots):
        _, exists, _ = near[j]
        if exists is not None:
            def clear(j=j):
                for n in range(ITERS):
                    foot_at[n, j] = jnp.zeros_like(foot_at[n, j])
                for n in range(ITERS):
                    times_at[n, j] = jnp.zeros_like(times_at[n, j])
                info_at[j] = jnp.zeros_like(info_at[j])
                cut[j] = jnp.zeros_like(cut[j])
            pl.when(jnp.logical_not(exists))(clear)

    for o in range(1, nz):
        back = lax.rem(iz + nz - o, nz)
        to_far(o, trace, trace_at.at[back], s_tr.at[o], r_tr.at[o]).wait_recv()
    pad = trace.shape[0]
    r = lax.broadcasted_iota(jnp.int32, (frames, nz * pad), 0)
    c = lax.broadcasted_iota(jnp.int32, (frames, nz * pad), 1)
    pick = ((r // local == c // pad) & (r % local == c % pad)).astype(F32)
    t = nn(pick, trace_at[...].reshape(nz * pad, lanes))
    info_at[0, 0:frames, :] = t
    info_at[0, frames:frames + 8, :] = idrow[...]
    spread(lambda j: info_at.at[0], lambda b: info_at.at[b], s_info, r_info)

    gather = (idcol[...] == placerow[0:1, :]).astype(BF16)
    a = lax.broadcasted_iota(jnp.int32, (lanes, lanes), 0)
    b = lax.broadcasted_iota(jnp.int32, (lanes, lanes), 1)
    fold = (a % owned == b % owned).astype(F32)
    central = rows * cols

    for n in range(ITERS):
        feet = foot_at[n, 0]
        update = jnp.zeros((frames, lanes), F32)
        same = []
        for j in range(slots):
            if n == 0 and j:
                await_near(j, info_at.at[j], s_info, r_info)
            if j:
                await_near(j, foot_at.at[n, j], s_foot.at[n], r_foot.at[n])
            same.append(idcol[...] == info_at[j, frames:frames + 1, :])
            tj = info_at[j, 0:frames, :] if n == 0 else times_at[n - 1, j]
            over = jnp.where(same[j], nt(feet, foot_at[n, j]), 0.0)
            update = update - nt(tj, over)
        if n == 0:
            own.wait()
            for o in range(1, nz):
                back = lax.rem(iz + nz - o, nz)
                to_far(o, movie.at[iz], seen.at[pl.ds(back * local, local)],
                       s_mov.at[o], r_mov.at[o]).wait_recv()
            for j, (dy, dx) in enumerate(dirs):
                if j == 0:
                    continue
                if dy:
                    start = 0 if dy < 0 else central - strip
                    if ny == 2:
                        start = jnp.where(iy == 0, central - strip, 0)
                    u = lax.broadcasted_iota(jnp.int32, (strip, central), 0) + start
                else:
                    column = 0 if dx < 0 else cols - 1
                    if nx == 2:
                        column = jnp.where(ix == 0, cols - 1, 0)
                    u = lax.broadcasted_iota(jnp.int32, (strip, central), 0) * cols + column
                v = lax.broadcasted_iota(jnp.int32, (strip, central), 1)
                choose = (u == v).astype(BF16)

                def body(f, carry, j=j, choose=choose):
                    cut[slots + j, f] = jnp.dot(
                        choose, seen[f], preferred_element_type=F32).astype(BF16)
                    return carry
                lax.fori_loop(0, frames, body, 0)
            spread(lambda j: cut.at[slots + j], lambda b: cut.at[b], s_cut, r_cut)
            for j in range(1, slots):
                await_near(j, cut.at[j], s_cut, r_cut)

            def collect(f, carry):
                got = jnp.dot(gather[:, 0:central], seen[f], preferred_element_type=F32)
                for j in range(1, slots):
                    at = central + (j - 1) * strip
                    got = got + jnp.dot(
                        gather[:, at:at + strip], cut[j, f], preferred_element_type=F32)
                patch[f] = got
                return carry
            lax.fori_loop(0, frames, collect, 0)
        energy = nt(jnp.ones((8, spot), F32), feet * feet)

        feet_t[...] = feet

        def inner(f, carry):
            numer[pl.ds(f, 1), :] = jnp.sum(
                jnp.transpose(feet_t[...] * patch[f]), axis=0, keepdims=True)
            return carry
        lax.fori_loop(0, frames, inner, 0)
        part_at[n, iz, 0:frames, :] = update + numer[...]
        part_at[n, iz, frames:frames + 8, :] = energy
        for o in range(1, nz):
            to_far(o, part_at.at[n, iz], part_at.at[n, iz], s_part.at[n, o], r_part.at[n, o]).start()
        for o in range(1, nz):
            back = lax.rem(iz + nz - o, nz)
            to_far(o, part_at.at[n, iz], part_at.at[n, back],
                   s_part.at[n, o], r_part.at[n, o]).wait_recv()
        total = part_at[n, 0]
        for z in range(1, nz):
            total = total + part_at[n, z]
        total = nn(total, fold)
        t = jnp.maximum(t + total[0:frames] / (total[frames:frames + 1] + RIDGE), 0.0)
        times_at[n, 0] = t
        spread(lambda j: times_at.at[n, 0], lambda b: times_at.at[n, b], s_time.at[n], r_time.at[n])
        wide = jnp.concatenate([t, jnp.zeros((128 - frames, lanes), F32)], axis=0)
        cols_t = jnp.transpose(wide)
        strength = jnp.sum(cols_t * cols_t, axis=1, keepdims=True)
        total_n = jnp.zeros((lanes, spot), F32)
        for f in range(frames):
            total_n = total_n + cols_t[:, f:f + 1] * patch[f]
        for j in range(slots):
            if j:
                await_near(j, times_at.at[n, j], s_time.at[n], r_time.at[n])
            both = jnp.where(same[j], nn(cols_t[:, 0:frames], times_at[n, j]), 0.0)
            total_n = total_n - nn(both, foot_at[n, j])
        feet = jnp.maximum(feet + total_n / (strength + RIDGE), 0.0)
        foot_at[n + 1, 0] = feet
        if n + 1 < ITERS:
            spread(lambda j: foot_at.at[n + 1, 0], lambda b: foot_at.at[n + 1, b],
                   s_foot.at[n + 1], r_foot.at[n + 1])

    trace_out[...] = t

    def block(o, s, z):
        first = pl.multiple_of((s * planes + z) * spot, spot)
        return to_far(o, foot_at.at[ITERS, 0, pl.ds(s * owned, owned)],
                      foot_out.at[:, pl.ds(first, spot)], s_out.at[o, s], r_out.at[o, s])

    for o in range(1, nz):
        for s in range(4):
            block(o, s, iz).start()
    for s in range(4):
        first = pl.multiple_of((s * planes + iz) * spot, spot)
        foot_out[:, pl.ds(first, spot)] = foot_at[ITERS, 0, s * owned:(s + 1) * owned, :]
    for o in range(1, nz):
        for s in range(4):
            block(o, s, lax.rem(iz + nz - o, nz)).wait_recv()
    for o in range(1, nz):
        to_far(o, trace, trace_at.at[iz], s_tr.at[o], r_tr.at[o]).wait_send()
        to_far(o, movie.at[iz], seen.at[pl.ds(iz * local, local)], s_mov.at[o], r_mov.at[o]).wait_send()
        for n in range(ITERS):
            to_far(o, part_at.at[n, iz], part_at.at[n, iz], s_part.at[n, o], r_part.at[n, o]).wait_send()
        for s in range(4):
            block(o, s, iz).wait_send()
    for j in range(1, slots):
        await_near(j, info_at.at[0], s_info, r_info, True)
        await_near(j, cut.at[slots + j], s_cut, r_cut, True)
        for n in range(ITERS):
            await_near(j, foot_at.at[n, 0], s_foot.at[n], r_foot.at[n], True)
            await_near(j, times_at.at[n, 0], s_time.at[n], r_time.at[n], True)


def shards(movie, footprints, traces, anchor_row, anchor_col):
    owned = footprints.shape[0]
    local, planes, height, breadth = movie.shape
    rows, cols = height // CELL, breadth // CELL
    spot = CELL * CELL
    ny, nx, nz = (lax.axis_size(a) for a in ("ty", "tx", "ta"))
    assert planes == nz
    frames, lanes = local * nz, 4 * owned
    cells = movie.reshape(local, planes, rows, CELL, cols, CELL).transpose(1, 0, 2, 4, 3, 5)
    cells = cells.reshape(planes, local, rows * cols, spot)
    width = cols * nx + 2
    iy, ix = lax.axis_index("ty"), lax.axis_index("tx")
    first = (anchor_row + 1 + iy * rows) * width + anchor_col + 1 + ix * cols
    offsets = jnp.array([0, 1, width, width + 1], dtype=jnp.int32)
    ids = (offsets[:, None] + first[None, :]).reshape(-1).astype(F32)
    strip = rows
    dirs = directions(ny, nx)
    slots = len(dirs)
    places = []
    for j, (dy, dx) in enumerate(dirs):
        ty = 1 - iy if dy and ny == 2 else iy + dy
        tx = 1 - ix if dx and nx == 2 else ix + dx
        if j == 0:
            within = jnp.arange(rows * cols)
        elif dy:
            below = (iy == 0) if ny == 2 else dy > 0
            within = jnp.arange(strip) + jnp.where(below, 0, rows * cols - strip)
        else:
            right = (ix == 0) if nx == 2 else dx > 0
            within = jnp.arange(strip) * cols + jnp.where(right, 0, cols - 1)
        places.append(
            (ty * rows + within // cols + 1) * width + tx * cols + within % cols + 1)
    place = jnp.concatenate(places).astype(F32)
    pad = -(-local // 8) * 8
    marks = jnp.zeros((pad, lanes), F32).at[:local].set(jnp.tile(traces, (1, 4)))
    dma = pltpu.SemaphoreType.DMA
    feet, marks = pl.pallas_call(
        functools.partial(kernel, (ny, nx, nz, rows, cols, local, planes, owned)),
        out_shape=(
            jax.ShapeDtypeStruct(footprints.shape, F32),
            jax.ShapeDtypeStruct((frames, lanes), F32),
        ),
        in_specs=[pl.BlockSpec(memory_space=pltpu.VMEM)] * 7,
        out_specs=[pl.BlockSpec(memory_space=pltpu.VMEM)] * 2,
        scratch_shapes=[
            pltpu.VMEM((frames, rows * cols, spot), BF16),
            pltpu.VMEM((2 * slots, frames, strip, spot), BF16),
            pltpu.VMEM((frames, lanes, spot), F32),
            pltpu.VMEM((ITERS + 1, slots, lanes, spot), F32),
            pltpu.VMEM((slots, frames + 8, lanes), F32),
            pltpu.VMEM((ITERS, slots, frames, lanes), F32),
            pltpu.VMEM((nz, pad, lanes), F32),
            pltpu.VMEM((ITERS, nz, frames + 8, lanes), F32),
            pltpu.VMEM((lanes, spot), F32),
            pltpu.VMEM((frames, lanes), F32),
            dma((nz,)), dma((nz,)),
            dma((slots,)), dma((slots,)),
            dma((ITERS, slots)), dma((ITERS, slots)),
            dma((nz,)), dma((nz,)),
            dma((slots,)), dma((slots,)),
            dma((ITERS, slots)), dma((ITERS, slots)),
            dma((ITERS, nz)), dma((ITERS, nz)),
            dma((nz, 4)), dma((nz, 4)),
            dma,
        ],
        compiler_params=pltpu.CompilerParams(
            collective_id=0, has_side_effects=True, vmem_limit_bytes=48 * 1024 * 1024
        ),
    )(
        cells, footprints, marks, jnp.broadcast_to(ids[None], (8, lanes)), ids[:, None],
        place[:, None], jnp.broadcast_to(place[None], (8, place.shape[0])),
    )
    return feet, lax.dynamic_slice(
        marks, (lax.axis_index("ta") * local, 0), (local, owned))


def solution(mesh):
    placed = (
        P("ta", None, "ty", "tx"),
        P(("ty", "tx"), None),
        P("ta", ("ty", "tx")),
        P(("ty", "tx")),
        P(("ty", "tx")),
    )
    return jax.shard_map(
        shards,
        mesh=mesh,
        in_specs=placed,
        out_specs=(P(("ty", "tx"), None), P("ta", ("ty", "tx"))),
        check_vma=False,
    )
```

```python
import functools

import jax
import jax.numpy as jnp
from jax import lax
from jax.experimental import pallas as pl
from jax.experimental.pallas import tpu as pltpu
from jax.sharding import PartitionSpec as P

CELL = 16
ITERS = 2
RIDGE = 1.0
HI = lax.Precision.HIGHEST
F32 = jnp.float32
BF16 = jnp.bfloat16
MESH = pl.DeviceIdType.MESH


def reach(count):
    return [0] if count == 1 else [0, 1] if count == 2 else [0, -1, 1]


def directions(mesh_y, mesh_x):
    return [(dy, dx) for dy in reach(mesh_y) for dx in reach(mesh_x)]


def shift(at, count, d):
    if d == 0:
        return at, None
    if count == 2:
        return 1 - at, None
    to = at + d
    return to, (to >= 0) & (to < count)


def opposite(d, count):
    return d if count == 2 else -d


def thirds(x):
    high = x.astype(BF16)
    rest = x - high.astype(F32)
    middle = rest.astype(BF16)
    return high, middle, (rest - middle.astype(F32)).astype(BF16)


def nt(a, b):
    return lax.dot_general(a, b, (((1,), (1,)), ((), ())), precision=HI, preferred_element_type=F32)


def nn(a, b):
    return jnp.dot(a, b, precision=HI, preferred_element_type=F32)


def kernel(
    sizes, movie, foot, trace, idrow, idcol, place, placerow,
    foot_out, trace_out,
    seen, cut, patch, foot_at, info_at, times_at, trace_at, part_at, feet_t, numer,
    s_mov, r_mov, s_cut, r_cut, s_foot, r_foot, s_tr, r_tr, s_info, r_info,
    s_time, r_time, s_part, r_part, s_out, r_out, l_sem,
):
    ny, nx, nz, rows, cols, local, planes, owned = sizes
    frames = local * nz
    spot = CELL * CELL
    lanes = 4 * owned
    strip = cut.shape[2]
    iy, ix, iz = lax.axis_index("ty"), lax.axis_index("tx"), lax.axis_index("ta")
    dirs = directions(ny, nx)
    slots = len(dirs)

    near = []
    for j, (dy, dx) in enumerate(dirs):
        ty, ey = shift(iy, ny, dy)
        tx, ex = shift(ix, nx, dx)
        exists = ey if ex is None else ex if ey is None else ey & ex
        back = dirs.index((opposite(dy, ny), opposite(dx, nx)))
        near.append(((ty, tx, iz), exists, back))

    def when(exists, act):
        if exists is None:
            act()
        else:
            pl.when(exists)(act)

    def far(o):
        return (iy, ix, lax.rem(iz + o, nz))

    def spread(src, dst, ssem, rsem):
        def go(j):
            device, exists, back = near[j]
            when(exists, lambda: pltpu.make_async_remote_copy(
                src_ref=src(j), dst_ref=dst(back), send_sem=ssem.at[j], recv_sem=rsem.at[back],
                device_id=device, device_id_type=MESH).start())
        for j in range(1, slots):
            go(j)

    def await_near(j, dst, ssem, rsem, send=False):
        device, exists, _ = near[j]

        def act():
            copy = pltpu.make_async_remote_copy(
                src_ref=dst, dst_ref=dst, send_sem=ssem.at[j], recv_sem=rsem.at[j],
                device_id=device, device_id_type=MESH)
            copy.wait_send() if send else copy.wait_recv()

        when(exists, act)

    def to_far(o, src, dst, ssem, rsem):
        return pltpu.make_async_remote_copy(
            src_ref=src, dst_ref=dst, send_sem=ssem, recv_sem=rsem,
            device_id=far(o), device_id_type=MESH)

    barrier = pltpu.get_barrier_semaphore()
    due = jnp.int32(nz - 1)
    for o in range(1, nz):
        pl.semaphore_signal(barrier, inc=1, device_id=far(o), device_id_type=MESH)
    for j in range(1, slots):
        device, exists, _ = near[j]
        when(exists, lambda device=device: pl.semaphore_signal(
            barrier, inc=1, device_id=device, device_id_type=MESH))
        due = due + (1 if exists is None else exists.astype(jnp.int32))
    pl.semaphore_wait(barrier, due)

    for o in range(1, nz):
        to_far(o, trace, trace_at.at[iz], s_tr.at[o], r_tr.at[o]).start()
    for o in range(1, nz):
        to_far(o, movie.at[lax.rem(iz + o, nz)], seen.at[pl.ds(iz * local, local)],
               s_mov.at[o], r_mov.at[o]).start()
    own = pltpu.make_async_copy(movie.at[iz], seen.at[pl.ds(iz * local, local)], l_sem)
    own.start()
    trace_at[iz] = trace[...]
    for s in range(4):
        first = pl.multiple_of((s * planes + iz) * spot, spot)
        foot_at[0, 0, s * owned:(s + 1) * owned, :] = foot[:, pl.ds(first, spot)]
    spread(lambda j: foot_at.at[0, 0], lambda b: foot_at.at[0, b], s_foot.at[0], r_foot.at[0])

    for j in range(1, slots):
        _, exists, _ = near[j]
        if exists is not None:
            def clear(j=j):
                for n in range(ITERS):
                    foot_at[n, j] = jnp.zeros_like(foot_at[n, j])
                for n in range(ITERS):
                    times_at[n, j] = jnp.zeros_like(times_at[n, j])
                info_at[j] = jnp.zeros_like(info_at[j])
                cut[j] = jnp.zeros_like(cut[j])
            pl.when(jnp.logical_not(exists))(clear)

    for o in range(1, nz):
        back = lax.rem(iz + nz - o, nz)
        to_far(o, trace, trace_at.at[back], s_tr.at[o], r_tr.at[o]).wait_recv()
    pad = trace.shape[0]
    r = lax.broadcasted_iota(jnp.int32, (frames, nz * pad), 0)
    c = lax.broadcasted_iota(jnp.int32, (frames, nz * pad), 1)
    pick = ((r // local == c // pad) & (r % local == c % pad)).astype(F32)
    t = nn(pick, trace_at[...].reshape(nz * pad, lanes))
    info_at[0, 0:frames, :] = t
    info_at[0, frames:frames + 8, :] = idrow[...]
    spread(lambda j: info_at.at[0], lambda b: info_at.at[b], s_info, r_info)

    gather = (idcol[...] == placerow[0:1, :]).astype(BF16)
    a = lax.broadcasted_iota(jnp.int32, (lanes, lanes), 0)
    b = lax.broadcasted_iota(jnp.int32, (lanes, lanes), 1)
    fold = (a % owned == b % owned).astype(F32)
    central = rows * cols

    for n in range(ITERS):
        feet = foot_at[n, 0]
        def met_movie():
            energy = nt(jnp.ones((8, spot), F32), feet * feet)

            feet_t[...] = feet

            def inner(f, carry):
                numer[pl.ds(f, 1), :] = jnp.sum(
                    jnp.transpose(feet_t[...] * patch[f]), axis=0, keepdims=True)
                return carry
            lax.fori_loop(0, frames, inner, 0)
            return energy

        if n:
            energy = met_movie()
        update = jnp.zeros((frames, lanes), F32)
        same = []
        for j in range(slots):
            if n == 0 and j:
                await_near(j, info_at.at[j], s_info, r_info)
            if j:
                await_near(j, foot_at.at[n, j], s_foot.at[n], r_foot.at[n])
            same.append(idcol[...] == info_at[j, frames:frames + 1, :])
            tj = info_at[j, 0:frames, :] if n == 0 else times_at[n - 1, j]
            over = jnp.where(same[j], nt(feet, foot_at[n, j]), 0.0)
            update = update - nt(tj, over)
        if n == 0:
            own.wait()
            for o in range(1, nz):
                back = lax.rem(iz + nz - o, nz)
                to_far(o, movie.at[iz], seen.at[pl.ds(back * local, local)],
                       s_mov.at[o], r_mov.at[o]).wait_recv()
            for j, (dy, dx) in enumerate(dirs):
                if j == 0:
                    continue
                if dy:
                    start = 0 if dy < 0 else central - strip
                    if ny == 2:
                        start = jnp.where(iy == 0, central - strip, 0)
                    u = lax.broadcasted_iota(jnp.int32, (strip, central), 0) + start
                else:
                    column = 0 if dx < 0 else cols - 1
                    if nx == 2:
                        column = jnp.where(ix == 0, cols - 1, 0)
                    u = lax.broadcasted_iota(jnp.int32, (strip, central), 0) * cols + column
                v = lax.broadcasted_iota(jnp.int32, (strip, central), 1)
                choose = (u == v).astype(BF16)

                def body(f, carry, j=j, choose=choose):
                    cut[slots + j, f] = jnp.dot(
                        choose, seen[f], preferred_element_type=F32).astype(BF16)
                    return carry
                lax.fori_loop(0, frames, body, 0)
            spread(lambda j: cut.at[slots + j], lambda b: cut.at[b], s_cut, r_cut)
            for j in range(1, slots):
                await_near(j, cut.at[j], s_cut, r_cut)

            def collect(f, carry):
                got = jnp.dot(gather[:, 0:central], seen[f], preferred_element_type=F32)
                for j in range(1, slots):
                    at = central + (j - 1) * strip
                    got = got + jnp.dot(
                        gather[:, at:at + strip], cut[j, f], preferred_element_type=F32)
                patch[f] = got
                return carry
            lax.fori_loop(0, frames, collect, 0)
        if n == 0:
            energy = met_movie()
        part_at[n, iz, 0:frames, :] = update + numer[...]
        part_at[n, iz, frames:frames + 8, :] = energy
        for o in range(1, nz):
            to_far(o, part_at.at[n, iz], part_at.at[n, iz], s_part.at[n, o], r_part.at[n, o]).start()
        for o in range(1, nz):
            back = lax.rem(iz + nz - o, nz)
            to_far(o, part_at.at[n, iz], part_at.at[n, back],
                   s_part.at[n, o], r_part.at[n, o]).wait_recv()
        total = part_at[n, 0]
        for z in range(1, nz):
            total = total + part_at[n, z]
        total = nn(total, fold)
        t = jnp.maximum(t + total[0:frames] / (total[frames:frames + 1] + RIDGE), 0.0)
        times_at[n, 0] = t
        spread(lambda j: times_at.at[n, 0], lambda b: times_at.at[n, b], s_time.at[n], r_time.at[n])
        wide = jnp.concatenate([t, jnp.zeros((128 - frames, lanes), F32)], axis=0)
        cols_t = jnp.transpose(wide)
        strength = jnp.sum(cols_t * cols_t, axis=1, keepdims=True)
        total_n = jnp.zeros((lanes, spot), F32)
        for f in range(frames):
            total_n = total_n + cols_t[:, f:f + 1] * patch[f]
        for j in range(slots):
            if j:
                await_near(j, times_at.at[n, j], s_time.at[n], r_time.at[n])
            both = jnp.where(same[j], nn(cols_t[:, 0:frames], times_at[n, j]), 0.0)
            total_n = total_n - nn(both, foot_at[n, j])
        feet = jnp.maximum(feet + total_n / (strength + RIDGE), 0.0)
        foot_at[n + 1, 0] = feet
        if n + 1 < ITERS:
            spread(lambda j: foot_at.at[n + 1, 0], lambda b: foot_at.at[n + 1, b],
                   s_foot.at[n + 1], r_foot.at[n + 1])

    trace_out[...] = t

    def block(o, s, z):
        first = pl.multiple_of((s * planes + z) * spot, spot)
        return to_far(o, foot_at.at[ITERS, 0, pl.ds(s * owned, owned)],
                      foot_out.at[:, pl.ds(first, spot)], s_out.at[o, s], r_out.at[o, s])

    for o in range(1, nz):
        for s in range(4):
            block(o, s, iz).start()
    for s in range(4):
        first = pl.multiple_of((s * planes + iz) * spot, spot)
        foot_out[:, pl.ds(first, spot)] = foot_at[ITERS, 0, s * owned:(s + 1) * owned, :]
    for o in range(1, nz):
        for s in range(4):
            block(o, s, lax.rem(iz + nz - o, nz)).wait_recv()
    for o in range(1, nz):
        to_far(o, trace, trace_at.at[iz], s_tr.at[o], r_tr.at[o]).wait_send()
        to_far(o, movie.at[iz], seen.at[pl.ds(iz * local, local)], s_mov.at[o], r_mov.at[o]).wait_send()
        for n in range(ITERS):
            to_far(o, part_at.at[n, iz], part_at.at[n, iz], s_part.at[n, o], r_part.at[n, o]).wait_send()
        for s in range(4):
            block(o, s, iz).wait_send()
    for j in range(1, slots):
        await_near(j, info_at.at[0], s_info, r_info, True)
        await_near(j, cut.at[slots + j], s_cut, r_cut, True)
        for n in range(ITERS):
            await_near(j, foot_at.at[n, 0], s_foot.at[n], r_foot.at[n], True)
            await_near(j, times_at.at[n, 0], s_time.at[n], r_time.at[n], True)


def shards(movie, footprints, traces, anchor_row, anchor_col):
    owned = footprints.shape[0]
    local, planes, height, breadth = movie.shape
    rows, cols = height // CELL, breadth // CELL
    spot = CELL * CELL
    ny, nx, nz = (lax.axis_size(a) for a in ("ty", "tx", "ta"))
    assert planes == nz
    frames, lanes = local * nz, 4 * owned
    cells = movie.reshape(local, planes, rows, CELL, cols, CELL).transpose(1, 0, 2, 4, 3, 5)
    cells = cells.reshape(planes, local, rows * cols, spot)
    width = cols * nx + 2
    iy, ix = lax.axis_index("ty"), lax.axis_index("tx")
    first = (anchor_row + 1 + iy * rows) * width + anchor_col + 1 + ix * cols
    offsets = jnp.array([0, 1, width, width + 1], dtype=jnp.int32)
    ids = (offsets[:, None] + first[None, :]).reshape(-1).astype(F32)
    strip = rows
    dirs = directions(ny, nx)
    slots = len(dirs)
    places = []
    for j, (dy, dx) in enumerate(dirs):
        ty = 1 - iy if dy and ny == 2 else iy + dy
        tx = 1 - ix if dx and nx == 2 else ix + dx
        if j == 0:
            within = jnp.arange(rows * cols)
        elif dy:
            below = (iy == 0) if ny == 2 else dy > 0
            within = jnp.arange(strip) + jnp.where(below, 0, rows * cols - strip)
        else:
            right = (ix == 0) if nx == 2 else dx > 0
            within = jnp.arange(strip) * cols + jnp.where(right, 0, cols - 1)
        places.append(
            (ty * rows + within // cols + 1) * width + tx * cols + within % cols + 1)
    place = jnp.concatenate(places).astype(F32)
    pad = -(-local // 8) * 8
    marks = jnp.zeros((pad, lanes), F32).at[:local].set(jnp.tile(traces, (1, 4)))
    dma = pltpu.SemaphoreType.DMA
    feet, marks = pl.pallas_call(
        functools.partial(kernel, (ny, nx, nz, rows, cols, local, planes, owned)),
        out_shape=(
            jax.ShapeDtypeStruct(footprints.shape, F32),
            jax.ShapeDtypeStruct((frames, lanes), F32),
        ),
        in_specs=[pl.BlockSpec(memory_space=pltpu.VMEM)] * 7,
        out_specs=[pl.BlockSpec(memory_space=pltpu.VMEM)] * 2,
        scratch_shapes=[
            pltpu.VMEM((frames, rows * cols, spot), BF16),
            pltpu.VMEM((2 * slots, frames, strip, spot), BF16),
            pltpu.VMEM((frames, lanes, spot), F32),
            pltpu.VMEM((ITERS + 1, slots, lanes, spot), F32),
            pltpu.VMEM((slots, frames + 8, lanes), F32),
            pltpu.VMEM((ITERS, slots, frames, lanes), F32),
            pltpu.VMEM((nz, pad, lanes), F32),
            pltpu.VMEM((ITERS, nz, frames + 8, lanes), F32),
            pltpu.VMEM((lanes, spot), F32),
            pltpu.VMEM((frames, lanes), F32),
            dma((nz,)), dma((nz,)),
            dma((slots,)), dma((slots,)),
            dma((ITERS, slots)), dma((ITERS, slots)),
            dma((nz,)), dma((nz,)),
            dma((slots,)), dma((slots,)),
            dma((ITERS, slots)), dma((ITERS, slots)),
            dma((ITERS, nz)), dma((ITERS, nz)),
            dma((nz, 4)), dma((nz, 4)),
            dma,
        ],
        compiler_params=pltpu.CompilerParams(
            collective_id=0, has_side_effects=True, vmem_limit_bytes=48 * 1024 * 1024
        ),
    )(
        cells, footprints, marks, jnp.broadcast_to(ids[None], (8, lanes)), ids[:, None],
        place[:, None], jnp.broadcast_to(place[None], (8, place.shape[0])),
    )
    return feet, lax.dynamic_slice(
        marks, (lax.axis_index("ta") * local, 0), (local, owned))


def solution(mesh):
    placed = (
        P("ta", None, "ty", "tx"),
        P(("ty", "tx"), None),
        P("ta", ("ty", "tx")),
        P(("ty", "tx")),
        P(("ty", "tx")),
    )
    return jax.shard_map(
        shards,
        mesh=mesh,
        in_specs=placed,
        out_specs=(P(("ty", "tx"), None), P("ta", ("ty", "tx"))),
        check_vma=False,
    )
```
